256 devices in a mesh: row: 16 (over x, y_hi, core), col: 16 (over z, y_lo).
Axes of the slice: x: 4, y: 4 (y_hi: 2, y_lo: 2; y = y_hi * 2 + y_lo), z: 8, core: 2. Of those that a mesh axis runs over, the one named last changes fastest.
Arguments:
- grad_iter: bfloat16 [7168, 9216], P('row', 'col'), may hold values from -0.02490811 to 0.02490811
Outputs:
- next_iter: bfloat16 [7168, 9216], P('row', 'col')
The draws below stay inside these ranges and needn't reach their ends.
All inputs are finite; a program needn't handle non-finite values.
Results may differ from the reference program's by a relative error of at most 0.025.
Values may be sent and summed in bfloat16 or wider, within the bound.
No kernel may reach another device: no remote copies, remote signals or barrier semaphores. Data moves between devices by JAX's collectives and lax.ppermute only.
A program may use at most 128 MiB of HBM per device.

```python
import jax
import jax.numpy as jnp
from jax import lax

DMODEL = 7168
DFF = 9216
N_COL = 16


def draw_grad_iter(key, part):
    key = jax.random.fold_in(key, 7)
    spread = 1.0 / (DFF ** 0.5 + DMODEL ** 0.5)
    values = jnp.clip(jax.random.normal(key, (DMODEL, DFF), jnp.float32), -4.47, 4.47) * spread
    return values.astype(jnp.bfloat16)


def setup_inputs(seed: int = 0) -> dict:
    key_of = jax.random.split(jax.random.key(seed), 2)
    return {
        "grad_iter": draw_grad_iter(jax.random.fold_in(key_of[1], 71), 0),
    }


linear_coef = 3.4445
cubic_coef = -4.7750
quintic_coef = 2.0315


def reference(grad_iter):
    col_width = DFF // N_COL
    gram_width = DMODEL // N_COL
    blocks = grad_iter.reshape(DMODEL, N_COL, col_width).transpose(1, 0, 2)

    def add_block(total, block):
        term = jnp.dot(block, block.T, preferred_element_type=jnp.float32).astype(jnp.bfloat16)
        term = lax.optimization_barrier(term)
        return total + term.astype(jnp.float32), None

    total, _ = lax.scan(add_block, jnp.zeros((DMODEL, DMODEL), jnp.float32), blocks)
    gram = total.astype(jnp.bfloat16)

    def add_poly(accum, index):
        start = (index * gram_width).astype(jnp.int32)
        columns = lax.dynamic_slice_in_dim(gram, start, gram_width, 1)
        term = quintic_coef * jnp.dot(columns, columns.T, preferred_element_type=jnp.float32)
        inside = lax.dynamic_slice_in_dim(term, start, gram_width, 1) + cubic_coef * columns.astype(jnp.float32)
        term = lax.dynamic_update_slice_in_dim(term, inside, start, 1)
        term = lax.optimization_barrier(term.astype(jnp.bfloat16))
        return accum + term.astype(jnp.float32), None

    summed, _ = lax.scan(add_poly, jnp.zeros((DMODEL, DMODEL), jnp.float32), jnp.arange(N_COL, dtype=jnp.int32))
    poly_matrix = summed.astype(jnp.bfloat16)
    newer = linear_coef * grad_iter.astype(jnp.float32) + jnp.dot(poly_matrix, grad_iter, preferred_element_type=jnp.float32)
    return (newer * (DFF ** 0.5)).astype(jnp.bfloat16)
```

```python
import jax
import jax.numpy as jnp
from jax import lax
from jax.sharding import PartitionSpec as P

DFF = 9216

linear_coef = 3.4445
cubic_coef = -4.775
quintic_coef = 2.0315

AXES = ("row", "col")
NX, NY, NZ, NC = 4, 4, 8, 2


def device_index(x, y, z, c):
    return ((x * 2 + y // 2) * 2 + c) * 16 + z * 2 + y % 2


def every_device():
    return [
        (x, y, z, c)
        for x in range(NX)
        for y in range(NY)
        for z in range(NZ)
        for c in range(NC)
    ]


def permute(value, target):
    pairs = []
    for x, y, z, c in every_device():
        tx, ty, tz, tc = target(x, y, z, c)
        pairs.append(
            (
                device_index(x, y, z, c),
                device_index(tx % NX, ty % NY, tz % NZ, tc % NC),
            )
        )
    return lax.ppermute(value, AXES, pairs)


def z_groups():
    groups = {}
    for x, y, z, c in every_device():
        groups.setdefault((x, y, c), []).append(device_index(x, y, z, c))
    return [groups[key] for key in sorted(groups)]


def along_x(k):
    return lambda x, y, z, c: (x + k, y, z, c)


def along_y(k):
    return lambda x, y, z, c: (x, y + k, z, c)


def along_first(k):
    return lambda x, y, z, c: (x, y + k, z, c) if c == 0 else (x + k, y, z, c)


def along_second(k):
    return lambda x, y, z, c: (x + k, y, z, c) if c == 0 else (x, y + k, z, c)


def other_core(x, y, z, c):
    return (x, y, z, 1 - c)


def swap_layout(x, y, z, c):
    return (x, (y // 2) * 2 + c, z, y % 2)


def dot(left, right, contract):
    return lax.dot_general(
        left, right, (((contract[0],), (contract[1],)), ((), ())),
        preferred_element_type=jnp.float32,
    )


def per_device(grad_iter):
    core = lax.axis_index("row") % NC
    home = permute(grad_iter, swap_layout)
    rows = home.shape[0]
    half = 2 * rows
    b1 = permute(home, along_x(-1))
    a1 = permute(home, along_y(-1))
    b3 = permute(home, along_x(1))
    a3 = permute(home, along_y(1))
    b2 = permute(home, along_x(2))
    a2 = permute(home, along_y(2))
    cols = jnp.concatenate([home, b1, b2, b3], axis=0)
    low = jnp.concatenate([home, a1], axis=0)
    high = jnp.concatenate([a2, a3], axis=0)
    mine = jnp.where(core == 0, low, high)
    other = jnp.where(core == 0, high, low)
    gram_other = dot(other, cols, (1, 1)).astype(jnp.bfloat16)
    received = permute(gram_other, other_core)
    gram_mine = (dot(mine, cols, (1, 1)) + received.astype(jnp.float32)).astype(jnp.bfloat16)
    groups = z_groups()
    part = lax.psum_scatter(
        gram_mine, AXES, scatter_dimension=0, axis_index_groups=groups, tiled=True
    )
    gram_mine = lax.all_gather(
        part, AXES, axis=0, axis_index_groups=groups, tiled=True
    )
    gram_other = permute(gram_mine, other_core)
    gram = jnp.concatenate([gram_mine, gram_other], axis=0)
    lines = jnp.concatenate([mine, other], axis=0)

    def split(value):
        return tuple(value[k * rows:(k + 1) * rows] for k in range(4))

    def first_product(_):
        return split(dot(gram, cols, (1, 0)).astype(jnp.bfloat16))

    def first_product_t(_):
        return split(dot(gram, lines, (0, 0)).astype(jnp.bfloat16))

    terms = lax.cond(core == 0, first_product, first_product_t, 0)
    got = [permute(terms[k], along_first(k)) for k in (1, 3, 2)]
    inner = terms[0].astype(jnp.float32)
    for value in got:
        inner = inner + value.astype(jnp.float32)
    inner_sent = inner.astype(jnp.bfloat16)
    g1 = permute(inner_sent, along_first(-1))
    g3 = permute(inner_sent, along_first(1))
    g2 = permute(inner_sent, along_first(2))

    def second_product(_):
        z = jnp.concatenate([inner_sent, g1, g2, g3], axis=0)
        return split(dot(gram, z, (0, 0)).astype(jnp.bfloat16))

    def second_product_t(_):
        z = jnp.concatenate([inner_sent, g1, g2, g3], axis=0)
        w = split(dot(gram, z, (1, 0)).astype(jnp.bfloat16))
        return (w[2], w[3], w[0], w[1])

    terms = lax.cond(core == 0, second_product, second_product_t, 0)
    got = [permute(terms[k], along_second(k)) for k in (1, 3, 2)]
    outer = terms[0].astype(jnp.float32)
    for value in got:
        outer = outer + value.astype(jnp.float32)
    newer = (
        linear_coef * home.astype(jnp.float32)
        + cubic_coef * inner
        + quintic_coef * outer
    )
    return permute((newer * DFF**0.5).astype(jnp.bfloat16), swap_layout)


def solution(mesh):
    placed = (P("row", "col"),)
    return jax.shard_map(
        per_device, mesh=mesh, in_specs=placed, out_specs=P("row", "col"), check_vma=False
    )
```

```python
import functools

import jax
import jax.numpy as jnp
from jax import lax
from jax.experimental import pallas as pl
from jax.experimental.pallas import tpu as pltpu
from jax.sharding import PartitionSpec as P

DFF = 9216

linear_coef = 3.4445
cubic_coef = -4.775
quintic_coef = 2.0315

AXES = ("row", "col")
NX, NY, NZ, NC = 4, 4, 8, 2


def device_index(x, y, z, c):
    return ((x * 2 + y // 2) * 2 + c) * 16 + z * 2 + y % 2


def every_device():
    return [
        (x, y, z, c)
        for x in range(NX)
        for y in range(NY)
        for z in range(NZ)
        for c in range(NC)
    ]


def permute(value, target):
    pairs = []
    for x, y, z, c in every_device():
        tx, ty, tz, tc = target(x, y, z, c)
        pairs.append(
            (
                device_index(x, y, z, c),
                device_index(tx % NX, ty % NY, tz % NZ, tc % NC),
            )
        )
    return lax.ppermute(value, AXES, pairs)


def z_groups():
    groups = {}
    for x, y, z, c in every_device():
        groups.setdefault((x, y, c), []).append(device_index(x, y, z, c))
    return [groups[key] for key in sorted(groups)]


def along_x(k):
    return lambda x, y, z, c: (x + k, y, z, c)


def along_y(k):
    return lambda x, y, z, c: (x, y + k, z, c)


def along_z(k):
    return lambda x, y, z, c: (x, y, z + k, c)


def along_first(k):
    return lambda x, y, z, c: (x, y + k, z, c) if c == 0 else (x + k, y, z, c)


def along_second(k):
    return lambda x, y, z, c: (x + k, y, z, c) if c == 0 else (x, y + k, z, c)


def other_core(x, y, z, c):
    return (x, y, z, 1 - c)


def swap_layout(x, y, z, c):
    return (x, (y // 2) * 2 + c, z, y % 2)


def dot(left, right, contract):
    return lax.dot_general(
        left, right, (((contract[0],), (contract[1],)), ((), ())),
        preferred_element_type=jnp.float32,
    )


def whole(count):
    return [pl.BlockSpec(memory_space=pltpu.VMEM)] * count


def call(kernel, place, inputs, out_shapes, scratch, flops):
    return pl.pallas_call(
        kernel,
        out_shape=[jax.ShapeDtypeStruct(shape, jnp.bfloat16) for shape in out_shapes],
        in_specs=[pl.BlockSpec(memory_space=pltpu.SMEM)] + whole(len(inputs)),
        out_specs=whole(len(out_shapes)),
        scratch_shapes=[pltpu.VMEM(shape, jnp.bfloat16) for shape in scratch],
        compiler_params=pltpu.CompilerParams(vmem_limit_bytes=48 * 1024 * 1024),
        cost_estimate=pl.CostEstimate(
            flops=flops,
            bytes_accessed=2 * sum(value.size for value in inputs),
            transcendentals=0,
        ),
    )(place, *inputs)


def stack_rows(target, pieces):
    rows = pieces[0].shape[0]
    for k, piece in enumerate(pieces):
        target[k * rows:(k + 1) * rows, :] = piece[...]


def roll_rows(z, target, pieces):
    rows = pieces[0].shape[0] * len(pieces) // NZ
    per_piece = NZ // len(pieces)
    for t in range(NZ):
        at = pl.multiple_of(lax.rem(t - z + NZ, NZ) * rows, 16)
        first = t % per_piece * rows
        target[pl.ds(at, rows), :] = pieces[t // per_piece][first:first + rows, :]


def gram_kernel(spans, place, home, b1, b2, b3, a1, a2, a3, sent, kept, cols, theirs, mine):
    stack_rows(cols, (home, b1, b2, b3))

    @pl.when(place[0] == 0)
    def _():
        roll_rows(place[1], mine, (home, a1))
        roll_rows(place[1], theirs, (a2, a3))

    @pl.when(place[0] != 0)
    def _():
        roll_rows(place[1], mine, (a2, a3))
        roll_rows(place[1], theirs, (home, a1))

    for rows, out in ((theirs, sent), (mine, kept)):
        at = 0
        for begin, end in spans:
            out[at:at + end - begin, :] = dot(rows[begin:end, :], cols[...], (1, 1)).astype(out.dtype)
            at += end - begin


def store_turned(value, outs):
    rows = outs[0].shape[0]
    value = value.T.astype(outs[0].dtype)
    for k, out in enumerate(outs):
        out[...] = value[k * rows:(k + 1) * rows, :]


def first_kernel(cuts, place, home, b1, b2, b3, a1, a2, a3, *refs):
    slices, outs, gram, stack = refs[:2 * len(cuts)], refs[-6:-2], refs[-2], refs[-1]
    depth = gram.shape[0] // 2
    for n, ref in enumerate(slices):
        k, first = cuts[n % len(cuts)]
        at = lax.rem(place[1] + k, NZ) * (depth // NZ) + (first + depth * (n // len(cuts)))
        gram[pl.ds(pl.multiple_of(at, 16), ref.shape[0]), :] = ref[...]

    @pl.when(place[0] == 0)
    def _():
        stack_rows(stack, (home, b1, b2, b3))
        store_turned(dot(stack[...], gram[...], (0, 1)), outs)

    @pl.when(place[0] != 0)
    def _():
        stack_rows(stack, (a2, a3, home, a1))
        store_turned(dot(stack[...], gram[...], (0, 0)), outs)


def second_kernel(place, gram, z0, z1, z2, z3, o0, o1, o2, o3, stack):
    stack_rows(stack, (z0, z1, z2, z3))

    @pl.when(place[0] == 0)
    def _():
        store_turned(dot(stack[...], gram[...], (0, 0)), (o0, o1, o2, o3))

    @pl.when(place[0] != 0)
    def _():
        store_turned(dot(stack[...], gram[...], (0, 1)), (o2, o3, o0, o1))


def reduce_z(term):
    half = NZ // 2
    cut = term(0).shape[0] // 32 * 16 + 16
    far = term(half)
    up = permute(far[:cut], along_z(1))
    down = permute(far[cut:], along_z(-1))
    total = term(0)
    for k in range(half - 1, 0, -1):
        above, up = lax.optimization_barrier((term(k), up))
        below, down = lax.optimization_barrier((term(NZ - k), down))
        if k == half - 1:
            above = jnp.concatenate(
                [add(above[:cut], up), above[cut:].astype(jnp.bfloat16)], axis=0
            )
            below = jnp.concatenate(
                [below[:cut].astype(jnp.bfloat16), add(below[cut:], down)], axis=0
            )
        else:
            above, below = add(above, up), add(below, down)
        up = permute(above, along_z(1))
        down = permute(below, along_z(-1))
    total = total + up.astype(jnp.float32) + down.astype(jnp.float32)
    return total.astype(jnp.bfloat16)


def add(left, right):
    return (left.astype(jnp.float32) + right.astype(jnp.float32)).astype(jnp.bfloat16)


def gather_z(part):
    up = down = part
    found = [(part, 0, 0)]
    for k in range(1, NZ // 2):
        up = permute(up, along_z(-1))
        down = permute(down, along_z(1))
        found += [(up, k, 0), (down, NZ - k, 0)]
    cut = part.shape[0] // 32 * 16 + 16
    found.append((permute(up[:cut], along_z(-1)), NZ // 2, 0))
    found.append((permute(down[cut:], along_z(1)), NZ // 2, cut))
    return [f[0] for f in found], [f[1:] for f in found]


def per_device(grad_iter):
    core = lax.axis_index("row") % NC
    place = jnp.stack([core, lax.axis_index("col") // 2]).astype(jnp.int32)
    home = permute(grad_iter, swap_layout)
    rows = home.shape[0]
    b1 = permute(home, along_x(-1))
    a1 = permute(home, along_y(-1))
    b3 = permute(home, along_x(1))
    a3 = permute(home, along_y(1))
    b2 = permute(home, along_x(2))
    a2 = permute(home, along_y(2))
    pieces = (home, b1, b2, b3, a1, a2, a3)
    width = 4 * rows
    half, part = width // 2, width // 2 // NZ
    flops = 2 * width * width * home.shape[1]
    near, far = 3 * part, 6 * part
    scratch = [(width, home.shape[1])] + [(half, home.shape[1])] * 2

    def terms_of(spans, place):
        size = sum(end - begin for begin, end in spans)
        sent, kept = call(
            functools.partial(gram_kernel, spans), place, pieces,
            [(size, width)] * 2, scratch, flops * size // half,
        )
        return kept, permute(sent, other_core)

    def sum_slice(pair, at):
        kept, received = (value[at:at + part].astype(jnp.float32) for value in pair)
        return kept + received

    middle = terms_of(((near, far),), place)
    farthest, later = lax.optimization_barrier(
        (sum_slice(middle, part).astype(jnp.bfloat16), place)
    )
    ends = terms_of(((0, near), (far, half)), later)

    def term(k):
        if k == NZ // 2:
            return farthest
        return sum_slice(middle if 3 <= k < 6 else ends, (k if k < 3 else k - 3) * part)

    sent_slices = []
    slices, cuts = gather_z(reduce_z(term))
    for n in range(len(slices)):
        value = slices[n]
        if n < len(slices) - 2:
            value = lax.optimization_barrier((value, slices[min(n + 2, len(slices) - 1)]))[0]
        sent_slices.append(permute(value, other_core))
    slices = slices + sent_slices
    *terms, gram = call(
        functools.partial(first_kernel, cuts), place, pieces + tuple(slices),
        [home.shape] * 4 + [(width, width)], [(width, home.shape[1])], flops,
    )
    got = [permute(terms[k], along_first(k)) for k in (1, 3, 2)]
    inner = terms[0].astype(jnp.float32)
    for value in got:
        inner = inner + value.astype(jnp.float32)
    inner_sent = inner.astype(jnp.bfloat16)
    g1 = permute(inner_sent, along_first(-1))
    g3 = permute(inner_sent, along_first(1))
    g2 = permute(inner_sent, along_first(2))

    terms = call(
        second_kernel, place, (gram, inner_sent, g1, g2, g3),
        [home.shape] * 4, [(width, home.shape[1])], flops,
    )
    got = [permute(terms[k], along_second(k)) for k in (1, 3, 2)]
    outer = terms[0].astype(jnp.float32)
    for value in got:
        outer = outer + value.astype(jnp.float32)
    newer = (
        linear_coef * home.astype(jnp.float32)
        + cubic_coef * inner
        + quintic_coef * outer
    )
    return permute((newer * DFF**0.5).astype(jnp.bfloat16), swap_layout)


def solution(mesh):
    placed = (P("row", "col"),)
    return jax.shard_map(
        per_device, mesh=mesh, in_specs=placed, out_specs=P("row", "col"), check_vma=False
    )
```

```python
import functools

import jax
import jax.numpy as jnp
from jax import lax
from jax.experimental import pallas as pl
from jax.experimental.pallas import tpu as pltpu
from jax.sharding import PartitionSpec as P

DFF = 9216

linear_coef = 3.4445
cubic_coef = -4.775
quintic_coef = 2.0315

AXES = ("row", "col")
NX, NY, NZ, NC = 4, 4, 8, 2


def after(value, *earlier):
    return lax.optimization_barrier((value,) + earlier)[0]


def device_index(x, y, z, c):
    return ((x * 2 + y // 2) * 2 + c) * 16 + z * 2 + y % 2


def every_device():
    return [
        (x, y, z, c)
        for x in range(NX)
        for y in range(NY)
        for z in range(NZ)
        for c in range(NC)
    ]


def permute(value, target):
    pairs = []
    for x, y, z, c in every_device():
        tx, ty, tz, tc = target(x, y, z, c)
        pairs.append(
            (
                device_index(x, y, z, c),
                device_index(tx % NX, ty % NY, tz % NZ, tc % NC),
            )
        )
    return lax.ppermute(value, AXES, pairs)


def z_groups():
    groups = {}
    for x, y, z, c in every_device():
        groups.setdefault((x, y, c), []).append(device_index(x, y, z, c))
    return [groups[key] for key in sorted(groups)]


def along_x(k):
    return lambda x, y, z, c: (x + k, y, z, c)


def along_y(k):
    return lambda x, y, z, c: (x, y + k, z, c)


def along_z(k):
    return lambda x, y, z, c: (x, y, z + k, c)


def along_first(k):
    return lambda x, y, z, c: (x, y + k, z, c) if c == 0 else (x + k, y, z, c)


def along_second(k):
    return lambda x, y, z, c: (x + k, y, z, c) if c == 0 else (x, y + k, z, c)


def other_core(x, y, z, c):
    return (x, y, z, 1 - c)


def swap_layout(x, y, z, c):
    return (x, (y // 2) * 2 + c, z, y % 2)


def dot(left, right, contract):
    return lax.dot_general(
        left, right, (((contract[0],), (contract[1],)), ((), ())),
        preferred_element_type=jnp.float32,
    )


def whole(count):
    return [pl.BlockSpec(memory_space=pltpu.VMEM)] * count


def call(kernel, place, inputs, out_shapes, scratch, flops):
    return pl.pallas_call(
        kernel,
        out_shape=[jax.ShapeDtypeStruct(shape, jnp.bfloat16) for shape in out_shapes],
        in_specs=[pl.BlockSpec(memory_space=pltpu.SMEM)] + whole(len(inputs)),
        out_specs=whole(len(out_shapes)),
        scratch_shapes=[pltpu.VMEM(shape, jnp.bfloat16) for shape in scratch],
        compiler_params=pltpu.CompilerParams(vmem_limit_bytes=24 * 1024 * 1024),
        cost_estimate=pl.CostEstimate(
            flops=flops,
            bytes_accessed=2 * sum(value.size for value in inputs),
            transcendentals=0,
        ),
    )(place, *inputs)


def stack_rows(target, pieces, lane=0):
    rows, width = pieces[0].shape
    for k, piece in enumerate(pieces):
        target[k * rows:(k + 1) * rows, lane:lane + width] = piece[...]


def roll_rows(z, target, pieces, lane):
    height, width = pieces[0].shape
    rows = height * len(pieces) // NZ
    per_piece = NZ // len(pieces)
    for t in range(NZ):
        at = pl.multiple_of(lax.rem(t - z + NZ, NZ) * rows, 16)
        first = t % per_piece * rows
        target[pl.ds(at, rows), lane:lane + width] = pieces[t // per_piece][first:first + rows, :]


def gram_kernel(place, *refs):
    home, f1, f2, f3, s1, s2, s3 = refs[:7]
    rhome, rf1, rf2, rf3, rs1, rs2, rs3 = refs[7:14]
    outs, (rows, cols) = refs[14:-2], refs[-2:]
    width = home.shape[1]
    lane = rows.shape[1] // 2
    for at in (0, lane):
        rows[:, at + width:at + lane] = jnp.zeros((rows.shape[0], lane - width), rows.dtype)
        cols[:, at + width:at + lane] = jnp.zeros((cols.shape[0], lane - width), cols.dtype)

    @pl.when(place[0] == 0)
    def _():
        roll_rows(place[1], rows, (home, f1), 0)
        roll_rows(place[1], rows, (rhome, rs1), lane)
        stack_rows(cols, (home, s1, s2, s3), 0)
        stack_rows(cols, (rhome, rf1, rf2, rf3), lane)

    @pl.when(place[0] != 0)
    def _():
        roll_rows(place[1], rows, (s2, s3), 0)
        roll_rows(place[1], rows, (rf2, rf3), lane)
        stack_rows(cols, (home, f1, f2, f3), 0)
        stack_rows(cols, (rhome, rs1, rs2, rs3), lane)

    value = dot(rows[...], cols[...], (1, 1)).astype(outs[0].dtype)
    at = 0
    for out in outs:
        out[...] = value[at:at + out.shape[0], :]
        at += out.shape[0]


def store_turned(value, outs):
    rows = outs[0].shape[0]
    value = value.T.astype(outs[0].dtype)
    for k, out in enumerate(outs):
        out[...] = value[k * rows:(k + 1) * rows, :]


def multiply(turned, gram, stack, outs):
    store_turned(dot(stack[...], gram[...], (0, 0 if turned else 1)), outs)


def first_kernel(cuts, span, place, home, s1, s2, s3, *refs):
    outs, gram, stack = refs[-6:-2], refs[-2], refs[-1]
    rows = gram.shape[0] // 2 // NZ
    for n, begin, size, k, first in cuts:
        at = pl.multiple_of(lax.rem(place[1] + k, NZ) * rows + first, 16)
        gram[pl.ds(at, size), :] = refs[n][begin:begin + size, :]
    next_kernel(span, place, gram, home, s1, s2, s3, *outs, stack)


def next_kernel(span, place, gram, home, s1, s2, s3, o0, o1, o2, o3, stack):
    home, s1, s2, s3 = (ref.at[:, span[0]:span[1]] for ref in (home, s1, s2, s3))

    @pl.when(place[0] == 0)
    def _():
        stack_rows(stack, (home, s1, s2, s3))
        multiply(False, gram, stack, (o0, o1, o2, o3))

    @pl.when(place[0] != 0)
    def _():
        stack_rows(stack, (s2, s3, home, s1))
        multiply(True, gram, stack, (o0, o1, o2, o3))


def second_kernel(place, gram, z0, z1, z2, z3, o0, o1, o2, o3, stack):
    stack_rows(stack, (z0, z1, z2, z3))

    @pl.when(place[0] == 0)
    def _():
        multiply(True, gram, stack, (o0, o1, o2, o3))

    @pl.when(place[0] != 0)
    def _():
        multiply(False, gram, stack, (o2, o3, o0, o1))


def near_far(rows):
    cut = rows // 32 * 16 + 16
    return cut, rows - cut


def reduce_z(terms):
    half = NZ // 2
    terms = list(terms[:half]) + [terms[half:half + 2]] + list(terms[half + 2:])
    up = permute(terms[half][0], along_z(1))
    down = permute(terms[half][1], along_z(-1))
    cut = up.shape[0]
    for k in range(half - 1, 0, -1):
        above, up = lax.optimization_barrier((terms[k], up))
        below, down = lax.optimization_barrier((terms[NZ - k], down))
        if k == half - 1:
            above = jnp.concatenate([add(above[:cut], up), above[cut:]], axis=0)
            below = jnp.concatenate([below[:cut], add(below[cut:], down)], axis=0)
        else:
            above, below = add(above, up), add(below, down)
        up = permute(above, along_z(1))
        down = permute(below, along_z(-1))
    total = terms[0].astype(jnp.float32) + up.astype(jnp.float32) + down.astype(jnp.float32)
    return total.astype(jnp.bfloat16)


def add(left, right):
    return (left.astype(jnp.float32) + right.astype(jnp.float32)).astype(jnp.bfloat16)


def gather_z(part):
    up = down = part
    steps = [(part,)]
    for k in range(1, NZ // 2):
        up = permute(up, along_z(-1))
        down = permute(down, along_z(1))
        steps.append((up, down))
    cut = near_far(part.shape[0])[0]
    steps.append((permute(up[:cut], along_z(-1)), permute(down[cut:], along_z(1))))
    rows = part.shape[0]
    places = [((0, 0),)] + [((k, 0), (NZ - k, 0)) for k in range(1, NZ // 2)]
    places.append(((NZ // 2, 0), (NZ // 2, cut)))
    steps = [steps[0] + steps[1]] + steps[2:]
    places = [places[0] + places[1]] + places[2:]
    sent = []
    for n, values in enumerate(steps):
        value = jnp.concatenate(values, axis=0)
        if n < len(steps) - 2:
            value = after(value, *steps[n + 1])
        sent.append(permute(value, other_core))
    own = [value for values in steps for value in values]
    cuts = []
    n = 0
    for values, where in zip(steps, places):
        for value, (k, first) in zip(values, where):
            cuts.append((n, 0, value.shape[0], k, first))
            n += 1
    for values, where in zip(steps, places):
        at = 0
        for value, (k, first) in zip(values, where):
            cuts.append((n, at, value.shape[0], k, first + rows * NZ))
            at += value.shape[0]
        n += 1
    return own + sent, cuts


def line_sum(terms, along):
    got = [permute(terms[k], along(k)) for k in (1, 3, 2)]
    total = terms[0].astype(jnp.float32)
    for value in got:
        total = total + value.astype(jnp.float32)
    return total


def per_device(grad_iter):
    core = lax.axis_index("row") % NC
    place = jnp.stack([core, lax.axis_index("col") // 2]).astype(jnp.int32)
    home = permute(grad_iter, swap_layout)
    rows = home.shape[0]
    f1 = permute(home, along_first(-1))
    s1 = permute(home, along_second(-1))
    f3 = permute(home, along_first(1))
    s3 = permute(home, along_second(1))
    f2 = permute(home, along_first(2))
    s2 = permute(after(home, f1), along_second(2))
    pieces = (home, f1, f2, f3, s1, s2, s3)
    others = [permute(after(value, f1, f2, f3, s1, s3), other_core) for value in pieces[:5]]
    others += [permute(s2, other_core), permute(after(s3, f1, f2, f3, s1), other_core)]
    width = 4 * rows
    half, part = width // 2, width // 2 // NZ
    flops = 2 * width * width * home.shape[1]
    lanes = (home.shape[1] + 127) // 128 * 256
    heights = [part] * 4 + list(near_far(part)) + [part] * 3
    terms = call(
        gram_kernel, place, list(pieces) + others, [(height, width) for height in heights],
        [(half, lanes), (width, lanes)], flops,
    )
    slices, cuts = gather_z(reduce_z(terms))
    middle = home.shape[1] // 256 * 128
    spans = ((0, middle), (middle, home.shape[1]))
    inner, outer, gram = [], [], None
    for span in spans:
        size = span[1] - span[0]
        shapes = [(rows, size)] * 4
        scratch = [(width, size)]
        work = flops * size // home.shape[1]
        if gram is None:
            *terms, gram = call(
                functools.partial(first_kernel, cuts, span), place,
                (home, s1, s2, s3) + tuple(slices), shapes + [(width, width)], scratch, work,
            )
        else:
            terms = call(
                functools.partial(next_kernel, span), place, (gram, home, s1, s2, s3),
                shapes, scratch, work,
            )
        inner.append(line_sum(terms, along_first))
    for value in inner:
        size = value.shape[1]
        sent = value.astype(jnp.bfloat16)
        g1 = permute(sent, along_first(-1))
        g3 = permute(sent, along_first(1))
        g2 = permute(sent, along_first(2))
        terms = call(
            second_kernel, place, (gram, sent, g1, g2, g3),
            [(rows, size)] * 4, [(width, size)], flops * size // home.shape[1],
        )
        outer.append(line_sum(terms, along_second))
    parts = []
    for (begin, end), once, twice in zip(spans, inner, outer):
        newer = (
            linear_coef * home[:, begin:end].astype(jnp.float32)
            + cubic_coef * once
            + quintic_coef * twice
        )
        parts.append(permute((newer * DFF**0.5).astype(jnp.bfloat16), swap_layout))
    return jnp.concatenate(parts, axis=1)


def solution(mesh):
    placed = (P("row", "col"),)
    return jax.shard_map(
        per_device, mesh=mesh, in_specs=placed, out_specs=P("row", "col"), check_vma=False
    )
```

```python
import functools

import jax
import jax.numpy as jnp
from jax import lax
from jax.experimental import pallas as pl
from jax.experimental.pallas import tpu as pltpu
from jax.sharding import PartitionSpec as P

DFF = 9216

linear_coef = 3.4445
cubic_coef = -4.775
quintic_coef = 2.0315

AXES = ("row", "col")
NX, NY, NZ, NC = 4, 4, 8, 2


def after(value, *earlier):
    return lax.optimization_barrier((value,) + earlier)[0]


def device_index(x, y, z, c):
    return ((x * 2 + y // 2) * 2 + c) * 16 + z * 2 + y % 2


def every_device():
    return [
        (x, y, z, c)
        for x in range(NX)
        for y in range(NY)
        for z in range(NZ)
        for c in range(NC)
    ]


def permute(value, target):
    pairs = []
    for x, y, z, c in every_device():
        tx, ty, tz, tc = target(x, y, z, c)
        pairs.append(
            (
                device_index(x, y, z, c),
                device_index(tx % NX, ty % NY, tz % NZ, tc % NC),
            )
        )
    return lax.ppermute(value, AXES, pairs)


def z_groups():
    groups = {}
    for x, y, z, c in every_device():
        groups.setdefault((x, y, c), []).append(device_index(x, y, z, c))
    return [groups[key] for key in sorted(groups)]


def along_x(k):
    return lambda x, y, z, c: (x + k, y, z, c)


def along_y(k):
    return lambda x, y, z, c: (x, y + k, z, c)


def along_z(k):
    return lambda x, y, z, c: (x, y, z + k, c)


def along_first(k):
    return lambda x, y, z, c: (x, y + k, z, c) if c == 0 else (x + k, y, z, c)


def along_second(k):
    return lambda x, y, z, c: (x + k, y, z, c) if c == 0 else (x, y + k, z, c)


def other_core(x, y, z, c):
    return (x, y, z, 1 - c)


def swap_layout(x, y, z, c):
    return (x, (y // 2) * 2 + c, z, y % 2)


def dot(left, right, contract):
    return lax.dot_general(
        left, right, (((contract[0],), (contract[1],)), ((), ())),
        preferred_element_type=jnp.float32,
    )


def whole(count):
    return [pl.BlockSpec(memory_space=pltpu.VMEM)] * count


def call(kernel, place, inputs, out_shapes, scratch, flops, room=10):
    return pl.pallas_call(
        kernel,
        out_shape=[jax.ShapeDtypeStruct(shape, jnp.bfloat16) for shape in out_shapes],
        in_specs=[pl.BlockSpec(memory_space=pltpu.SMEM)] + whole(len(inputs)),
        out_specs=whole(len(out_shapes)),
        scratch_shapes=[pltpu.VMEM(shape, jnp.bfloat16) for shape in scratch],
        compiler_params=pltpu.CompilerParams(vmem_limit_bytes=room * 1024 * 1024),
        cost_estimate=pl.CostEstimate(
            flops=flops,
            bytes_accessed=2 * sum(value.size for value in inputs),
            transcendentals=0,
        ),
    )(place, *inputs)


def stack_rows(target, pieces, lane=0):
    rows, width = pieces[0].shape
    for k, piece in enumerate(pieces):
        target[k * rows:(k + 1) * rows, lane:lane + width] = piece[...]


def roll_rows(z, target, pieces, lane):
    height, width = pieces[0].shape
    rows = height * len(pieces) // NZ
    per_piece = NZ // len(pieces)
    for t in range(NZ):
        at = pl.multiple_of(lax.rem(t - z + NZ, NZ) * rows, 16)
        first = t % per_piece * rows
        target[pl.ds(at, rows), lane:lane + width] = pieces[t // per_piece][first:first + rows, :]


def gram_kernel(place, *refs):
    home, f1, f2, f3, s1, s2, s3 = refs[:7]
    rhome, rf1, rf2, rf3, rs1, rs2, rs3 = refs[7:14]
    outs, (rows, cols) = refs[14:-2], refs[-2:]
    width = home.shape[1]
    lane = rows.shape[1] // 2
    for at in (0, lane):
        rows[:, at + width:at + lane] = jnp.zeros((rows.shape[0], lane - width), rows.dtype)
        cols[:, at + width:at + lane] = jnp.zeros((cols.shape[0], lane - width), cols.dtype)

    @pl.when(place[0] == 0)
    def _():
        roll_rows(place[1], rows, (home, f1), 0)
        roll_rows(place[1], rows, (rhome, rs1), lane)
        stack_rows(cols, (home, s1, s2, s3), 0)
        stack_rows(cols, (rhome, rf1, rf2, rf3), lane)

    @pl.when(place[0] != 0)
    def _():
        roll_rows(place[1], rows, (s2, s3), 0)
        roll_rows(place[1], rows, (rf2, rf3), lane)
        stack_rows(cols, (home, f1, f2, f3), 0)
        stack_rows(cols, (rhome, rs1, rs2, rs3), lane)

    half = rows.shape[0] // 2
    for part in (0, half):
        value = dot(rows[part:part + half, :], cols[...], (1, 1)).astype(outs[0].dtype)
        at = 0
        for out in outs:
            if part <= at < part + half:
                out[...] = value[at - part:at - part + out.shape[0], :]
            at += out.shape[0]


def store_turned(value, outs):
    rows = outs[0].shape[0]
    value = value.T.astype(outs[0].dtype)
    for k, out in enumerate(outs):
        out[...] = value[k * rows:(k + 1) * rows, :]


def multiply(turned, gram, stack, outs):
    store_turned(dot(stack[...], gram[...], (0, 0 if turned else 1)), outs)


def first_kernel(cuts, span, place, home, s1, s2, s3, *refs):
    outs, gram, stack = refs[-6:-2], refs[-2], refs[-1]
    rows = gram.shape[0] // 2 // NZ
    for n, begin, size, k, first in cuts:
        at = pl.multiple_of(lax.rem(place[1] + k, NZ) * rows + first, 16)
        gram[pl.ds(at, size), :] = refs[n][begin:begin + size, :]
    next_kernel(span, place, gram, home, s1, s2, s3, *outs, stack)


def next_kernel(span, place, gram, home, s1, s2, s3, o0, o1, o2, o3, stack):
    home, s1, s2, s3 = (ref.at[:, span[0]:span[1]] for ref in (home, s1, s2, s3))

    @pl.when(place[0] == 0)
    def _():
        stack_rows(stack, (home, s1, s2, s3))
        multiply(False, gram, stack, (o0, o1, o2, o3))

    @pl.when(place[0] != 0)
    def _():
        stack_rows(stack, (s2, s3, home, s1))
        multiply(True, gram, stack, (o0, o1, o2, o3))


def second_kernel(place, gram, z0, z1, z2, z3, o0, o1, o2, o3, stack):
    stack_rows(stack, (z0, z1, z2, z3))

    @pl.when(place[0] == 0)
    def _():
        multiply(True, gram, stack, (o0, o1, o2, o3))

    @pl.when(place[0] != 0)
    def _():
        multiply(False, gram, stack, (o2, o3, o0, o1))


def near_far(rows):
    cut = rows // 32 * 16 + 16
    return cut, rows - cut


def reduce_z(terms):
    half = NZ // 2
    terms = list(terms[:half]) + [terms[half:half + 2]] + list(terms[half + 2:])
    up = permute(terms[half][0], along_z(1))
    down = permute(terms[half][1], along_z(-1))
    cut = up.shape[0]
    for k in range(half - 1, 0, -1):
        above, up = lax.optimization_barrier((terms[k], up))
        below, down = lax.optimization_barrier((terms[NZ - k], down))
        if k == half - 1:
            above = jnp.concatenate([add(above[:cut], up), above[cut:]], axis=0)
            below = jnp.concatenate([below[:cut], add(below[cut:], down)], axis=0)
        else:
            above, below = add(above, up), add(below, down)
        up = permute(above, along_z(1))
        down = permute(below, along_z(-1))
    total = terms[0].astype(jnp.float32) + up.astype(jnp.float32) + down.astype(jnp.float32)
    return total.astype(jnp.bfloat16)


def add(left, right):
    return (left.astype(jnp.float32) + right.astype(jnp.float32)).astype(jnp.bfloat16)


def gather_z(part):
    up = down = part
    steps = [(part,)]
    for k in range(1, NZ // 2):
        up = permute(up, along_z(-1))
        down = permute(down, along_z(1))
        steps.append((up, down))
    cut = near_far(part.shape[0])[0]
    steps.append((permute(up[:cut], along_z(-1)), permute(down[cut:], along_z(1))))
    rows = part.shape[0]
    places = [((0, 0),)] + [((k, 0), (NZ - k, 0)) for k in range(1, NZ // 2)]
    places.append(((NZ // 2, 0), (NZ // 2, cut)))
    steps = [steps[0] + steps[1]] + steps[2:]
    places = [places[0] + places[1]] + places[2:]
    sent = []
    for n, values in enumerate(steps):
        value = jnp.concatenate(values, axis=0)
        if n < len(steps) - 2:
            value = after(value, *steps[n + 1])
        sent.append(permute(value, other_core))
    own = [value for values in steps for value in values]
    cuts = []
    n = 0
    for values, where in zip(steps, places):
        for value, (k, first) in zip(values, where):
            cuts.append((n, 0, value.shape[0], k, first))
            n += 1
    for values, where in zip(steps, places):
        at = 0
        for value, (k, first) in zip(values, where):
            cuts.append((n, at, value.shape[0], k, first + rows * NZ))
            at += value.shape[0]
        n += 1
    return own + sent, cuts


def line_sum(terms, along):
    got = [permute(terms[k], along(k)) for k in (1, 3, 2)]
    total = terms[0].astype(jnp.float32)
    for value in got:
        total = total + value.astype(jnp.float32)
    return total


def per_device(grad_iter):
    core = lax.axis_index("row") % NC
    place = jnp.stack([core, lax.axis_index("col") // 2]).astype(jnp.int32)
    home = permute(after(grad_iter, place), swap_layout)
    rows = home.shape[0]
    f1 = permute(home, along_first(-1))
    s1 = permute(home, along_second(-1))
    f3 = permute(home, along_first(1))
    s3 = permute(home, along_second(1))
    f2 = permute(home, along_first(2))
    s2 = permute(after(home, f1), along_second(2))
    pieces = (home, f1, f2, f3, s1, s2, s3)
    others = [permute(after(value, f1, f3), other_core) for value in (home, f1)]
    others += [permute(value, other_core) for value in pieces[2:]]
    width = 4 * rows
    half, part = width // 2, width // 2 // NZ
    flops = 2 * width * width * home.shape[1]
    lanes = (home.shape[1] + 127) // 128 * 256
    heights = [part] * 4 + list(near_far(part)) + [part] * 3
    terms = call(
        gram_kernel, place, list(pieces) + others, [(height, width) for height in heights],
        [(half, lanes), (width, lanes)], flops, 13,
    )
    slices, cuts = gather_z(reduce_z(terms))
    middle = home.shape[1] // 256 * 128
    spans = ((middle, home.shape[1]), (0, middle))
    inner, outer, gram = [], [], None
    for span in spans:
        size = span[1] - span[0]
        shapes = [(rows, size)] * 4
        scratch = [(width, size)]
        work = flops * size // home.shape[1]
        if gram is None:
            *terms, gram = call(
                functools.partial(first_kernel, cuts, span), place,
                (home, s1, s2, s3) + tuple(slices), shapes + [(width, width)], scratch, work,
            )
        else:
            terms = call(
                functools.partial(next_kernel, span), place, (gram, home, s1, s2, s3),
                shapes, scratch, work,
            )
        inner.append(line_sum(terms, along_first))
    for value in inner:
        size = value.shape[1]
        sent = value.astype(jnp.bfloat16)
        g1 = permute(sent, along_first(-1))
        g3 = permute(sent, along_first(1))
        g2 = permute(sent, along_first(2))
        terms = call(
            second_kernel, place, (gram, sent, g1, g2, g3),
            [(rows, size)] * 4, [(width, size)], flops * size // home.shape[1],
        )
        outer.append(line_sum(terms, along_second))
    parts = []
    for (begin, end), once, twice in zip(spans, inner, outer):
        newer = (
            linear_coef * home[:, begin:end].astype(jnp.float32)
            + cubic_coef * once
            + quintic_coef * twice
        )
        parts.append(permute((newer * DFF**0.5).astype(jnp.bfloat16), swap_layout))
    return jnp.concatenate(parts[::-1], axis=1)


def solution(mesh):
    placed = (P("row", "col"),)
    return jax.shard_map(
        per_device, mesh=mesh, in_specs=placed, out_specs=P("row", "col"), check_vma=False
    )
```

```python
import functools

import jax
import jax.numpy as jnp
from jax import lax
from jax.experimental import pallas as pl
from jax.experimental.pallas import tpu as pltpu
from jax.sharding import PartitionSpec as P

DFF = 9216

linear_coef = 3.4445
cubic_coef = -4.775
quintic_coef = 2.0315

AXES = ("row", "col")
NX, NY, NZ, NC = 4, 4, 8, 2


def after(value, *earlier):
    return lax.optimization_barrier((value,) + earlier)[0]


def device_index(x, y, z, c):
    return ((x * 2 + y // 2) * 2 + c) * 16 + z * 2 + y % 2


def every_device():
    return [
        (x, y, z, c)
        for x in range(NX)
        for y in range(NY)
        for z in range(NZ)
        for c in range(NC)
    ]


def permute(value, target):
    pairs = []
    for x, y, z, c in every_device():
        tx, ty, tz, tc = target(x, y, z, c)
        pairs.append(
            (
                device_index(x, y, z, c),
                device_index(tx % NX, ty % NY, tz % NZ, tc % NC),
            )
        )
    return lax.ppermute(value, AXES, pairs)


def z_groups():
    groups = {}
    for x, y, z, c in every_device():
        groups.setdefault((x, y, c), []).append(device_index(x, y, z, c))
    return [groups[key] for key in sorted(groups)]


def along_x(k):
    return lambda x, y, z, c: (x + k, y, z, c)


def along_y(k):
    return lambda x, y, z, c: (x, y + k, z, c)


def along_z(k):
    return lambda x, y, z, c: (x, y, z + k, c)


def along_first(k):
    return lambda x, y, z, c: (x, y + k, z, c) if c == 0 else (x + k, y, z, c)


def along_second(k):
    return lambda x, y, z, c: (x + k, y, z, c) if c == 0 else (x, y + k, z, c)


def other_core(x, y, z, c):
    return (x, y, z, 1 - c)


def swap_layout(x, y, z, c):
    return (x, (y // 2) * 2 + c, z, y % 2)


def dot(left, right, contract):
    return lax.dot_general(
        left, right, (((contract[0],), (contract[1],)), ((), ())),
        preferred_element_type=jnp.float32,
    )


def whole(count):
    return [pl.BlockSpec(memory_space=pltpu.VMEM)] * count


def call(kernel, place, inputs, out_shapes, scratch, flops, room=10):
    return pl.pallas_call(
        kernel,
        out_shape=[jax.ShapeDtypeStruct(shape, jnp.bfloat16) for shape in out_shapes],
        in_specs=[pl.BlockSpec(memory_space=pltpu.SMEM)] + whole(len(inputs)),
        out_specs=whole(len(out_shapes)),
        scratch_shapes=[pltpu.VMEM(shape, jnp.bfloat16) for shape in scratch],
        compiler_params=pltpu.CompilerParams(vmem_limit_bytes=room * 1024 * 1024),
        cost_estimate=pl.CostEstimate(
            flops=flops,
            bytes_accessed=2 * sum(value.size for value in inputs),
            transcendentals=0,
        ),
    )(place, *inputs)


def stack_rows(target, pieces, lane=0):
    rows, width = pieces[0].shape
    for k, piece in enumerate(pieces):
        target[k * rows:(k + 1) * rows, lane:lane + width] = piece[...]


def roll_rows(z, target, pieces, lane):
    height, width = pieces[0].shape
    rows = height * len(pieces) // NZ
    per_piece = NZ // len(pieces)
    for t in range(NZ):
        at = pl.multiple_of(lax.rem(t - z + NZ, NZ) * rows, 16)
        first = t % per_piece * rows
        target[pl.ds(at, rows), lane:lane + width] = pieces[t // per_piece][first:first + rows, :]


def gram_kernel(place, *refs):
    home, f1, f2, f3, s1, s2, s3 = refs[:7]
    rhome, rf1, rf2, rf3, rs1, rs2, rs3 = refs[7:14]
    outs, (rows, cols) = refs[14:-2], refs[-2:]
    width = home.shape[1]
    lane = rows.shape[1] // 2
    for at in (0, lane):
        rows[:, at + width:at + lane] = jnp.zeros((rows.shape[0], lane - width), rows.dtype)
        cols[:, at + width:at + lane] = jnp.zeros((cols.shape[0], lane - width), cols.dtype)

    @pl.when(place[0] == 0)
    def _():
        roll_rows(place[1], rows, (home, f1), 0)
        roll_rows(place[1], rows, (rhome, rs1), lane)
        stack_rows(cols, (home, s1, s2, s3), 0)
        stack_rows(cols, (rhome, rf1, rf2, rf3), lane)

    @pl.when(place[0] != 0)
    def _():
        roll_rows(place[1], rows, (s2, s3), 0)
        roll_rows(place[1], rows, (rf2, rf3), lane)
        stack_rows(cols, (home, f1, f2, f3), 0)
        stack_rows(cols, (rhome, rs1, rs2, rs3), lane)

    half = rows.shape[0] // 2
    for part in (0, half):
        value = dot(rows[part:part + half, :], cols[...], (1, 1)).astype(outs[0].dtype)
        at = 0
        for out in outs:
            if part <= at < part + half:
                out[...] = value[at - part:at - part + out.shape[0], :]
            at += out.shape[0]


def store_turned(value, outs):
    rows = outs[0].shape[0]
    value = value.T.astype(outs[0].dtype)
    for k, out in enumerate(outs):
        out[...] = value[k * rows:(k + 1) * rows, :]


def multiply(turned, gram, stack, outs):
    store_turned(dot(stack[...], gram[...], (0, 0 if turned else 1)), outs)


def first_kernel(cuts, span, place, home, s1, s2, s3, *refs):
    outs, gram, stack = refs[-6:-2], refs[-2], refs[-1]
    rows = gram.shape[0] // 2 // NZ
    for n, begin, size, k, first in cuts:
        at = pl.multiple_of(lax.rem(place[1] + k, NZ) * rows + first, 16)
        gram[pl.ds(at, size), :] = refs[n][begin:begin + size, :]
    next_kernel(span, place, gram, home, s1, s2, s3, *outs, stack)


def next_kernel(span, place, gram, home, s1, s2, s3, o0, o1, o2, o3, stack):
    home, s1, s2, s3 = (ref.at[:, span[0]:span[1]] for ref in (home, s1, s2, s3))

    @pl.when(place[0] == 0)
    def _():
        stack_rows(stack, (home, s1, s2, s3))
        multiply(False, gram, stack, (o0, o1, o2, o3))

    @pl.when(place[0] != 0)
    def _():
        stack_rows(stack, (s2, s3, home, s1))
        multiply(True, gram, stack, (o0, o1, o2, o3))


def second_kernel(place, gram, z0, z1, z2, z3, o0, o1, o2, o3, stack):
    stack_rows(stack, (z0, z1, z2, z3))

    @pl.when(place[0] == 0)
    def _():
        multiply(True, gram, stack, (o0, o1, o2, o3))

    @pl.when(place[0] != 0)
    def _():
        multiply(False, gram, stack, (o2, o3, o0, o1))


def near_far(rows):
    cut = rows // 32 * 16 + 16
    return cut, rows - cut


def reduce_z(terms):
    half = NZ // 2
    terms = list(terms[:half]) + [terms[half:half + 2]] + list(terms[half + 2:])
    up = permute(terms[half][0], along_z(1))
    down = permute(terms[half][1], along_z(-1))
    cut = up.shape[0]
    for k in range(half - 1, 0, -1):
        above, up = lax.optimization_barrier((terms[k], up))
        below, down = lax.optimization_barrier((terms[NZ - k], down))
        if k == half - 1:
            above = jnp.concatenate([add(above[:cut], up), above[cut:]], axis=0)
            below = jnp.concatenate([below[:cut], add(below[cut:], down)], axis=0)
        else:
            above, below = add(above, up), add(below, down)
        up = permute(above, along_z(1))
        down = permute(below, along_z(-1))
    total = terms[0].astype(jnp.float32) + up.astype(jnp.float32) + down.astype(jnp.float32)
    return total.astype(jnp.bfloat16)


def add(left, right):
    return (left.astype(jnp.float32) + right.astype(jnp.float32)).astype(jnp.bfloat16)


def gather_z(part):
    up = down = part
    steps = [(part,)]
    for k in range(1, NZ // 2):
        up = permute(up, along_z(-1))
        down = permute(down, along_z(1))
        steps.append((up, down))
    cut = near_far(part.shape[0])[0]
    steps.append((permute(up[:cut], along_z(-1)), permute(down[cut:], along_z(1))))
    rows = part.shape[0]
    places = [((0, 0),)] + [((k, 0), (NZ - k, 0)) for k in range(1, NZ // 2)]
    places.append(((NZ // 2, 0), (NZ // 2, cut)))
    steps = [steps[0] + steps[1]] + steps[2:]
    places = [places[0] + places[1]] + places[2:]
    sent = []
    for n, values in enumerate(steps):
        value = jnp.concatenate(values, axis=0)
        if n < len(steps) - 2:
            value = after(value, *steps[n + 1])
        sent.append(permute(value, other_core))
    own = [value for values in steps for value in values]
    cuts = []
    n = 0
    for values, where in zip(steps, places):
        for value, (k, first) in zip(values, where):
            cuts.append((n, 0, value.shape[0], k, first))
            n += 1
    for values, where in zip(steps, places):
        at = 0
        for value, (k, first) in zip(values, where):
            cuts.append((n, at, value.shape[0], k, first + rows * NZ))
            at += value.shape[0]
        n += 1
    return own + sent, cuts


def line_sum(terms, along):
    got = [permute(terms[k], along(k)) for k in (1, 3, 2)]
    total = terms[0].astype(jnp.float32)
    for value in got:
        total = total + value.astype(jnp.float32)
    return total


def per_device(grad_iter):
    core = lax.axis_index("row") % NC
    place = jnp.stack([core, lax.axis_index("col") // 2]).astype(jnp.int32)
    home = permute(after(grad_iter, place), swap_layout)
    rows = home.shape[0]
    f1 = permute(home, along_first(-1))
    s1 = permute(home, along_second(-1))
    f3 = permute(home, along_first(1))
    s3 = permute(home, along_second(1))
    f2 = permute(home, along_first(2))
    s2 = permute(home, along_second(2))
    pieces = (home, f1, f2, f3, s1, s2, s3)
    others = [permute(after(value, f2, f3), other_core) for value in pieces[:4]]
    others += [permute(value, other_core) for value in pieces[4:]]
    width = 4 * rows
    half, part = width // 2, width // 2 // NZ
    flops = 2 * width * width * home.shape[1]
    lanes = (home.shape[1] + 127) // 128 * 256
    heights = [part] * 4 + list(near_far(part)) + [part] * 3
    terms = call(
        gram_kernel, place, list(pieces) + others, [(height, width) for height in heights],
        [(half, lanes), (width, lanes)], flops, 13,
    )
    slices, cuts = gather_z(reduce_z(terms))
    middle = home.shape[1] // 256 * 128
    spans = ((middle, home.shape[1]), (0, middle))
    inner, outer, gram = [], [], None
    for span in spans:
        size = span[1] - span[0]
        shapes = [(rows, size)] * 4
        scratch = [(width, size)]
        work = flops * size // home.shape[1]
        if gram is None:
            *terms, gram = call(
                functools.partial(first_kernel, cuts, span), place,
                (home, s1, s2, s3) + tuple(slices), shapes + [(width, width)], scratch, work,
            )
        else:
            terms = call(
                functools.partial(next_kernel, span), place, (gram, home, s1, s2, s3),
                shapes, scratch, work,
            )
        inner.append(line_sum(terms, along_first))
    for value in inner:
        size = value.shape[1]
        sent = value.astype(jnp.bfloat16)
        g1 = permute(sent, along_first(-1))
        g3 = permute(sent, along_first(1))
        g2 = permute(sent, along_first(2))
        terms = call(
            second_kernel, place, (gram, sent, g1, g2, g3),
            [(rows, size)] * 4, [(width, size)], flops * size // home.shape[1],
        )
        outer.append(line_sum(terms, along_second))
    parts = []
    for (begin, end), once, twice in zip(spans, inner, outer):
        newer = (
            linear_coef * home[:, begin:end].astype(jnp.float32)
            + cubic_coef * once
            + quintic_coef * twice
        )
        parts.append(permute((newer * DFF**0.5).astype(jnp.bfloat16), swap_layout))
    return jnp.concatenate(parts[::-1], axis=1)


def solution(mesh):
    placed = (P("row", "col"),)
    return jax.shard_map(
        per_device, mesh=mesh, in_specs=placed, out_specs=P("row", "col"), check_vma=False
    )
```

```python
import functools

import jax
import jax.numpy as jnp
from jax import lax
from jax.experimental import pallas as pl
from jax.experimental.pallas import tpu as pltpu
from jax.sharding import PartitionSpec as P

DFF = 9216

linear_coef = 3.4445
cubic_coef = -4.775
quintic_coef = 2.0315

AXES = ("row", "col")
NX, NY, NZ, NC = 4, 4, 8, 2


def after(value, *earlier):
    return lax.optimization_barrier((value,) + earlier)[0]


def device_index(x, y, z, c):
    return ((x * 2 + y // 2) * 2 + c) * 16 + z * 2 + y % 2


def every_device():
    return [
        (x, y, z, c)
        for x in range(NX)
        for y in range(NY)
        for z in range(NZ)
        for c in range(NC)
    ]


def permute(value, target):
    pairs = []
    for x, y, z, c in every_device():
        tx, ty, tz, tc = target(x, y, z, c)
        pairs.append(
            (
                device_index(x, y, z, c),
                device_index(tx % NX, ty % NY, tz % NZ, tc % NC),
            )
        )
    return lax.ppermute(value, AXES, pairs)


def z_groups():
    groups = {}
    for x, y, z, c in every_device():
        groups.setdefault((x, y, c), []).append(device_index(x, y, z, c))
    return [groups[key] for key in sorted(groups)]


def along_x(k):
    return lambda x, y, z, c: (x + k, y, z, c)


def along_y(k):
    return lambda x, y, z, c: (x, y + k, z, c)


def along_z(k):
    return lambda x, y, z, c: (x, y, z + k, c)


def along_first(k):
    return lambda x, y, z, c: (x, y + k, z, c) if c == 0 else (x + k, y, z, c)


def along_second(k):
    return lambda x, y, z, c: (x + k, y, z, c) if c == 0 else (x, y + k, z, c)


def other_core(x, y, z, c):
    return (x, y, z, 1 - c)


def swap_layout(x, y, z, c):
    return (x, (y // 2) * 2 + c, z, y % 2)


def dot(left, right, contract):
    return lax.dot_general(
        left, right, (((contract[0],), (contract[1],)), ((), ())),
        preferred_element_type=jnp.float32,
    )


def whole(count):
    return [pl.BlockSpec(memory_space=pltpu.VMEM)] * count


def call(kernel, place, inputs, out_shapes, scratch, flops, room=10):
    return pl.pallas_call(
        kernel,
        out_shape=[jax.ShapeDtypeStruct(shape, jnp.bfloat16) for shape in out_shapes],
        in_specs=[pl.BlockSpec(memory_space=pltpu.SMEM)] + whole(len(inputs)),
        out_specs=whole(len(out_shapes)),
        scratch_shapes=[pltpu.VMEM(shape, jnp.bfloat16) for shape in scratch],
        compiler_params=pltpu.CompilerParams(vmem_limit_bytes=room * 1024 * 1024),
        cost_estimate=pl.CostEstimate(
            flops=flops,
            bytes_accessed=2 * sum(value.size for value in inputs),
            transcendentals=0,
        ),
    )(place, *inputs)


def stack_rows(target, pieces, lane=0):
    rows, width = pieces[0].shape
    for k, piece in enumerate(pieces):
        target[k * rows:(k + 1) * rows, lane:lane + width] = piece[...]


def roll_rows(z, target, pieces, lane):
    height, width = pieces[0].shape
    rows = height * len(pieces) // NZ
    per_piece = NZ // len(pieces)
    for t in range(NZ):
        at = pl.multiple_of(lax.rem(t - z + NZ, NZ) * rows, 16)
        first = t % per_piece * rows
        target[pl.ds(at, rows), lane:lane + width] = pieces[t // per_piece][first:first + rows, :]


def gram_kernel(place, home, f1, f2, f3, s1, s2, s3, *refs):
    before, outs, (rows, cols) = refs[:-2][:1], refs[:-2], refs[-2:]
    f, g = (f1, f2, f3), (s1, s2, s3)
    if len(outs) > 1:
        outs, f, g = outs[1:], g, f
    else:
        before = ()

    @pl.when(place[0] == 0)
    def _():
        roll_rows(place[1], rows, (home, f[0]), 0)
        stack_rows(cols, (home,) + g, 0)

    @pl.when(place[0] != 0)
    def _():
        roll_rows(place[1], rows, (g[1], g[2]), 0)
        stack_rows(cols, (home,) + f, 0)

    half = rows.shape[0] // 2
    for part in (0, half):
        value = dot(rows[part:part + half, :], cols[...], (1, 1))
        for ref in before:
            value = value + ref[part:part + half, :].astype(jnp.float32)
        value = value.astype(outs[0].dtype)
        at = 0
        for out in outs:
            begin, end = max(at, part), min(at + out.shape[0], part + half)
            if begin < end:
                out[begin - at:end - at, :] = value[begin - part:end - part, :]
            at += out.shape[0]


def store_turned(value, outs):
    rows = outs[0].shape[0]
    value = value.T.astype(outs[0].dtype)
    for k, out in enumerate(outs):
        out[...] = value[k * rows:(k + 1) * rows, :]


def multiply(turned, gram, stack, outs):
    store_turned(dot(stack[...], gram[...], (0, 0 if turned else 1)), outs)


def first_kernel(cuts, span, place, home, s1, s2, s3, *refs):
    outs, gram, stack = refs[-6:-2], refs[-2], refs[-1]
    rows = gram.shape[0] // 2 // NZ
    for n, begin, size, k, first in cuts:
        at = pl.multiple_of(lax.rem(place[1] + k, NZ) * rows + first, 16)
        gram[pl.ds(at, size), :] = refs[n][begin:begin + size, :]
    next_kernel(span, place, gram, home, s1, s2, s3, *outs, stack)


def next_kernel(span, place, gram, home, s1, s2, s3, o0, o1, o2, o3, stack):
    home, s1, s2, s3 = (ref.at[:, span[0]:span[1]] for ref in (home, s1, s2, s3))

    @pl.when(place[0] == 0)
    def _():
        stack_rows(stack, (home, s1, s2, s3))
        multiply(False, gram, stack, (o0, o1, o2, o3))

    @pl.when(place[0] != 0)
    def _():
        stack_rows(stack, (s2, s3, home, s1))
        multiply(True, gram, stack, (o0, o1, o2, o3))


def second_kernel(place, gram, z0, z1, z2, z3, o0, o1, o2, o3, stack):
    stack_rows(stack, (z0, z1, z2, z3))

    @pl.when(place[0] == 0)
    def _():
        multiply(True, gram, stack, (o0, o1, o2, o3))

    @pl.when(place[0] != 0)
    def _():
        multiply(False, gram, stack, (o2, o3, o0, o1))


def near_far(rows):
    cut = rows // 32 * 16 + 16
    return cut, rows - cut


def reduce_z(terms):
    half = NZ // 2
    terms = list(terms[:half]) + [terms[half:half + 2]] + list(terms[half + 2:])
    up = permute(terms[half][0], along_z(1))
    down = permute(terms[half][1], along_z(-1))
    cut = up.shape[0]
    for k in range(half - 1, 0, -1):
        above, up = lax.optimization_barrier((terms[k], up))
        below, down = lax.optimization_barrier((terms[NZ - k], down))
        if k == half - 1:
            above = jnp.concatenate([add(above[:cut], up), above[cut:]], axis=0)
            below = jnp.concatenate([below[:cut], add(below[cut:], down)], axis=0)
        else:
            above, below = add(above, up), add(below, down)
        up = permute(above, along_z(1))
        down = permute(below, along_z(-1))
    total = terms[0].astype(jnp.float32) + up.astype(jnp.float32) + down.astype(jnp.float32)
    return total.astype(jnp.bfloat16)


def add(left, right):
    return (left.astype(jnp.float32) + right.astype(jnp.float32)).astype(jnp.bfloat16)


def gather_z(part):
    up = down = part
    steps = [(part,)]
    for k in range(1, NZ // 2):
        up = permute(up, along_z(-1))
        down = permute(down, along_z(1))
        steps.append((up, down))
    cut = near_far(part.shape[0])[0]
    steps.append((permute(up[:cut], along_z(-1)), permute(down[cut:], along_z(1))))
    rows = part.shape[0]
    places = [((0, 0),)] + [((k, 0), (NZ - k, 0)) for k in range(1, NZ // 2)]
    places.append(((NZ // 2, 0), (NZ // 2, cut)))
    steps = [steps[0] + steps[1]] + steps[2:]
    places = [places[0] + places[1]] + places[2:]
    sent = []
    for n, values in enumerate(steps):
        value = jnp.concatenate(values, axis=0)
        if n < len(steps) - 2:
            value = after(value, *steps[n + 1])
        sent.append(permute(value, other_core))
    own = [value for values in steps for value in values]
    cuts = []
    n = 0
    for values, where in zip(steps, places):
        for value, (k, first) in zip(values, where):
            cuts.append((n, 0, value.shape[0], k, first))
            n += 1
    for values, where in zip(steps, places):
        at = 0
        for value, (k, first) in zip(values, where):
            cuts.append((n, at, value.shape[0], k, first + rows * NZ))
            at += value.shape[0]
        n += 1
    return own + sent, cuts


def line_sum(terms, along):
    got = [permute(terms[k], along(k)) for k in (1, 3, 2)]
    total = terms[0].astype(jnp.float32)
    for value in got:
        total = total + value.astype(jnp.float32)
    return total


def per_device(grad_iter):
    core = lax.axis_index("row") % NC
    place = jnp.stack([core, lax.axis_index("col") // 2]).astype(jnp.int32)
    home = permute(after(grad_iter, place), swap_layout)
    rows = home.shape[0]
    f1 = permute(home, along_first(-1))
    s1 = permute(home, along_second(-1))
    f3 = permute(home, along_first(1))
    s3 = permute(home, along_second(1))
    f2 = permute(home, along_first(2))
    s2 = permute(home, along_second(2))
    pieces = (home, f1, f2, f3, s1, s2, s3)
    others = [permute(after(value, f1, f2, f3, s3), other_core) for value in pieces[:4]]
    others += [permute(value, other_core) for value in pieces[4:]]
    width = 4 * rows
    half, part = width // 2, width // 2 // NZ
    flops = 2 * width * width * home.shape[1]
    heights = [part] * 4 + list(near_far(part)) + [part] * 3
    scratch = [(half, home.shape[1]), (width, home.shape[1])]
    own, = call(gram_kernel, place, pieces, [(half, width)], scratch, flops // 2, 10)
    terms = call(
        gram_kernel, place, tuple(others) + (own,), [(height, width) for height in heights],
        scratch, flops // 2, 10,
    )
    slices, cuts = gather_z(reduce_z(terms))
    middle = home.shape[1] // 256 * 128
    spans = ((middle, home.shape[1]), (0, middle))
    inner, outer, gram = [], [], None
    for span in spans:
        size = span[1] - span[0]
        shapes = [(rows, size)] * 4
        scratch = [(width, size)]
        work = flops * size // home.shape[1]
        if gram is None:
            *terms, gram = call(
                functools.partial(first_kernel, cuts, span), place,
                (home, s1, s2, s3) + tuple(slices), shapes + [(width, width)], scratch, work,
            )
        else:
            terms = call(
                functools.partial(next_kernel, span), place, (gram, home, s1, s2, s3),
                shapes, scratch, work,
            )
        inner.append(line_sum(terms, along_first))
    for value in inner:
        size = value.shape[1]
        sent = value.astype(jnp.bfloat16)
        g1 = permute(sent, along_first(-1))
        g3 = permute(sent, along_first(1))
        g2 = permute(sent, along_first(2))
        terms = call(
            second_kernel, place, (gram, sent, g1, g2, g3),
            [(rows, size)] * 4, [(width, size)], flops * size // home.shape[1],
        )
        outer.append(line_sum(terms, along_second))
    parts = []
    for (begin, end), once, twice in zip(spans, inner, outer):
        newer = (
            linear_coef * home[:, begin:end].astype(jnp.float32)
            + cubic_coef * once
            + quintic_coef * twice
        )
        parts.append(permute((newer * DFF**0.5).astype(jnp.bfloat16), swap_layout))
    return jnp.concatenate(parts[::-1], axis=1)


def solution(mesh):
    placed = (P("row", "col"),)
    return jax.shard_map(
        per_device, mesh=mesh, in_specs=placed, out_specs=P("row", "col"), check_vma=False
    )
```

```python
import functools

import jax
import jax.numpy as jnp
from jax import lax
from jax.experimental import pallas as pl
from jax.experimental.pallas import tpu as pltpu
from jax.sharding import PartitionSpec as P

DFF = 9216

linear_coef = 3.4445
cubic_coef = -4.775
quintic_coef = 2.0315

AXES = ("row", "col")
NX, NY, NZ, NC = 4, 4, 8, 2


def after(value, *earlier):
    return lax.optimization_barrier((value,) + earlier)[0]


def device_index(x, y, z, c):
    return ((x * 2 + y // 2) * 2 + c) * 16 + z * 2 + y % 2


def every_device():
    return [
        (x, y, z, c)
        for x in range(NX)
        for y in range(NY)
        for z in range(NZ)
        for c in range(NC)
    ]


def permute(value, target):
    pairs = []
    for x, y, z, c in every_device():
        tx, ty, tz, tc = target(x, y, z, c)
        pairs.append(
            (
                device_index(x, y, z, c),
                device_index(tx % NX, ty % NY, tz % NZ, tc % NC),
            )
        )
    return lax.ppermute(value, AXES, pairs)


def z_groups():
    groups = {}
    for x, y, z, c in every_device():
        groups.setdefault((x, y, c), []).append(device_index(x, y, z, c))
    return [groups[key] for key in sorted(groups)]


def along_x(k):
    return lambda x, y, z, c: (x + k, y, z, c)


def along_y(k):
    return lambda x, y, z, c: (x, y + k, z, c)


def along_z(k):
    return lambda x, y, z, c: (x, y, z + k, c)


def along_first(k):
    return lambda x, y, z, c: (x, y + k, z, c) if c == 0 else (x + k, y, z, c)


def along_second(k):
    return lambda x, y, z, c: (x + k, y, z, c) if c == 0 else (x, y + k, z, c)


def other_core(x, y, z, c):
    return (x, y, z, 1 - c)


def swap_layout(x, y, z, c):
    return (x, (y // 2) * 2 + c, z, y % 2)


def dot(left, right, contract):
    return lax.dot_general(
        left, right, (((contract[0],), (contract[1],)), ((), ())),
        preferred_element_type=jnp.float32,
    )


def whole(count):
    return [pl.BlockSpec(memory_space=pltpu.VMEM)] * count


def call(kernel, place, inputs, out_shapes, scratch, flops, room=10):
    return pl.pallas_call(
        kernel,
        out_shape=[jax.ShapeDtypeStruct(shape, jnp.bfloat16) for shape in out_shapes],
        in_specs=[pl.BlockSpec(memory_space=pltpu.SMEM)] + whole(len(inputs)),
        out_specs=whole(len(out_shapes)),
        scratch_shapes=[pltpu.VMEM(shape, jnp.bfloat16) for shape in scratch],
        compiler_params=pltpu.CompilerParams(vmem_limit_bytes=room * 1024 * 1024),
        cost_estimate=pl.CostEstimate(
            flops=flops,
            bytes_accessed=2 * sum(value.size for value in inputs),
            transcendentals=0,
        ),
    )(place, *inputs)


def stack_rows(target, pieces, lane=0):
    rows, width = pieces[0].shape
    for k, piece in enumerate(pieces):
        target[k * rows:(k + 1) * rows, lane:lane + width] = piece[...]


def roll_rows(z, target, pieces, lane):
    height, width = pieces[0].shape
    rows = height * len(pieces) // NZ
    per_piece = NZ // len(pieces)
    for t in range(NZ):
        at = pl.multiple_of(lax.rem(t - z + NZ, NZ) * rows, 16)
        first = t % per_piece * rows
        target[pl.ds(at, rows), lane:lane + width] = pieces[t // per_piece][first:first + rows, :]


def gram_kernel(place, home, f1, f2, f3, s1, s2, s3, *refs):
    before, outs, (rows, cols) = refs[:-2][:1], refs[:-2], refs[-2:]
    f, g = (f1, f2, f3), (s1, s2, s3)
    if len(outs) > 1:
        outs, f, g = outs[1:], g, f
    else:
        before = ()

    @pl.when(place[0] == 0)
    def _():
        roll_rows(place[1], rows, (home, f[0]), 0)
        stack_rows(cols, (home,) + g, 0)

    @pl.when(place[0] != 0)
    def _():
        roll_rows(place[1], rows, (g[1], g[2]), 0)
        stack_rows(cols, (home,) + f, 0)

    half = rows.shape[0] // 2
    for part in (0, half):
        value = dot(rows[part:part + half, :], cols[...], (1, 1))
        for ref in before:
            value = value + ref[part:part + half, :].astype(jnp.float32)
        value = value.astype(outs[0].dtype)
        at = 0
        for out in outs:
            begin, end = max(at, part), min(at + out.shape[0], part + half)
            if begin < end:
                out[begin - at:end - at, :] = value[begin - part:end - part, :]
            at += out.shape[0]


def store_turned(value, outs):
    rows = outs[0].shape[0]
    value = value.T.astype(outs[0].dtype)
    for k, out in enumerate(outs):
        out[...] = value[k * rows:(k + 1) * rows, :]


def multiply(turned, gram, stack, outs):
    store_turned(dot(stack[...], gram[...], (0, 0 if turned else 1)), outs)


def first_kernel(cuts, span, place, home, s1, s2, s3, *refs):
    outs, gram, stack = refs[-6:-2], refs[-2], refs[-1]
    rows = gram.shape[0] // 2 // NZ
    for n, begin, size, k, first in cuts:
        at = pl.multiple_of(lax.rem(place[1] + k, NZ) * rows + first, 16)
        gram[pl.ds(at, size), :] = refs[n][begin:begin + size, :]
    next_kernel(span, place, gram, home, s1, s2, s3, *outs, stack)


def next_kernel(span, place, gram, home, s1, s2, s3, o0, o1, o2, o3, stack):
    home, s1, s2, s3 = (ref.at[:, span[0]:span[1]] for ref in (home, s1, s2, s3))

    @pl.when(place[0] == 0)
    def _():
        stack_rows(stack, (home, s1, s2, s3))
        multiply(False, gram, stack, (o0, o1, o2, o3))

    @pl.when(place[0] != 0)
    def _():
        stack_rows(stack, (s2, s3, home, s1))
        multiply(True, gram, stack, (o0, o1, o2, o3))


def second_kernel(place, gram, z0, z1, z2, z3, o0, o1, o2, o3, stack):
    stack_rows(stack, (z0, z1, z2, z3))

    @pl.when(place[0] == 0)
    def _():
        multiply(True, gram, stack, (o0, o1, o2, o3))

    @pl.when(place[0] != 0)
    def _():
        multiply(False, gram, stack, (o2, o3, o0, o1))


def near_far(rows):
    cut = rows // 32 * 16 + 16
    return cut, rows - cut


def reduce_z(terms):
    half = NZ // 2
    terms = list(terms[:half]) + [terms[half:half + 2]] + list(terms[half + 2:])
    up = permute(terms[half][0], along_z(1))
    down = permute(terms[half][1], along_z(-1))
    cut = up.shape[0]
    for k in range(half - 1, 0, -1):
        above, up = lax.optimization_barrier((terms[k], up))
        below, down = lax.optimization_barrier((terms[NZ - k], down))
        if k == half - 1:
            above = jnp.concatenate([add(above[:cut], up), above[cut:]], axis=0)
            below = jnp.concatenate([below[:cut], add(below[cut:], down)], axis=0)
        else:
            above, below = add(above, up), add(below, down)
        up = permute(above, along_z(1))
        down = permute(below, along_z(-1))
    total = terms[0].astype(jnp.float32) + up.astype(jnp.float32) + down.astype(jnp.float32)
    return total.astype(jnp.bfloat16)


def add(left, right):
    return (left.astype(jnp.float32) + right.astype(jnp.float32)).astype(jnp.bfloat16)


def gather_z(part):
    up = down = part
    steps = [(part,)]
    for k in range(1, NZ // 2):
        up = permute(up, along_z(-1))
        down = permute(down, along_z(1))
        steps.append((up, down))
    cut = near_far(part.shape[0])[0]
    steps.append((permute(up[:cut], along_z(-1)), permute(down[cut:], along_z(1))))
    rows = part.shape[0]
    places = [((0, 0),)] + [((k, 0), (NZ - k, 0)) for k in range(1, NZ // 2)]
    places.append(((NZ // 2, 0), (NZ // 2, cut)))
    steps = [steps[0] + steps[1]] + steps[2:]
    places = [places[0] + places[1]] + places[2:]
    sent = []
    for n, values in enumerate(steps):
        value = jnp.concatenate(values, axis=0)
        if n < len(steps) - 2:
            value = after(value, *steps[n + 1])
        sent.append(permute(value, other_core))
    own = [value for values in steps for value in values]
    cuts = []
    n = 0
    for values, where in zip(steps, places):
        for value, (k, first) in zip(values, where):
            cuts.append((n, 0, value.shape[0], k, first))
            n += 1
    for values, where in zip(steps, places):
        at = 0
        for value, (k, first) in zip(values, where):
            cuts.append((n, at, value.shape[0], k, first + rows * NZ))
            at += value.shape[0]
        n += 1
    return own + sent, cuts


def line_sum(terms, along):
    got = [permute(terms[k], along(k)) for k in (1, 3, 2)]
    total = terms[0].astype(jnp.float32)
    for value in got:
        total = total + value.astype(jnp.float32)
    return total


def per_device(grad_iter):
    core = lax.axis_index("row") % NC
    place = jnp.stack([core, lax.axis_index("col") // 2]).astype(jnp.int32)
    home = permute(after(grad_iter, place), swap_layout)
    rows = home.shape[0]
    f1 = permute(home, along_first(-1))
    s1 = permute(home, along_second(-1))
    f3 = permute(home, along_first(1))
    s3 = permute(home, along_second(1))
    f2 = permute(home, along_first(2))
    s2 = permute(home, along_second(2))
    pieces = (home, f1, f2, f3, s1, s2, s3)
    others = [permute(after(value, f1, f2, f3), other_core) for value in pieces[:4]]
    others += [permute(value, other_core) for value in pieces[4:]]
    width = 4 * rows
    half, part = width // 2, width // 2 // NZ
    flops = 2 * width * width * home.shape[1]
    heights = [part] * 4 + list(near_far(part)) + [part] * 3
    scratch = [(half, home.shape[1]), (width, home.shape[1])]
    own, = call(gram_kernel, place, pieces, [(half, width)], scratch, flops // 2, 10)
    terms = call(
        gram_kernel, place, tuple(others) + (own,), [(height, width) for height in heights],
        scratch, flops // 2, 10,
    )
    slices, cuts = gather_z(reduce_z(terms))
    middle = home.shape[1] // 256 * 128
    spans = ((middle, home.shape[1]), (0, middle))
    inner, outer, gram = [], [], None
    for span in spans:
        size = span[1] - span[0]
        shapes = [(rows, size)] * 4
        scratch = [(width, size)]
        work = flops * size // home.shape[1]
        if gram is None:
            *terms, gram = call(
                functools.partial(first_kernel, cuts, span), place,
                (home, s1, s2, s3) + tuple(slices), shapes + [(width, width)], scratch, work,
            )
        else:
            terms = call(
                functools.partial(next_kernel, span), place, (gram, home, s1, s2, s3),
                shapes, scratch, work,
            )
        inner.append(line_sum(terms, along_first))
    for value in inner:
        size = value.shape[1]
        sent = value.astype(jnp.bfloat16)
        g1 = permute(sent, along_first(-1))
        g3 = permute(sent, along_first(1))
        g2 = permute(sent, along_first(2))
        terms = call(
            second_kernel, place, (gram, sent, g1, g2, g3),
            [(rows, size)] * 4, [(width, size)], flops * size // home.shape[1],
        )
        outer.append(line_sum(terms, along_second))
    parts = []
    for (begin, end), once, twice in zip(spans, inner, outer):
        newer = (
            linear_coef * home[:, begin:end].astype(jnp.float32)
            + cubic_coef * once
            + quintic_coef * twice
        )
        parts.append(permute((newer * DFF**0.5).astype(jnp.bfloat16), swap_layout))
    return jnp.concatenate(parts[::-1], axis=1)


def solution(mesh):
    placed = (P("row", "col"),)
    return jax.shard_map(
        per_device, mesh=mesh, in_specs=placed, out_specs=P("row", "col"), check_vma=False
    )
```
